32 devices in a mesh: row: 16 (over z, x, core), rhs: 2 (over y).
Axes of the slice: x: 2, y: 2, z: 4, core: 2. Of those that a mesh axis runs over, the one named last changes fastest.
Arguments:
- rhs_in: float32 [2, 128, 8192], P(None, ('rhs', 'row')), may hold values from -6 to 6
- pivots: int32 [8192], replicated, may hold values from 0 to 8191, each once
- owners: int32 [16], replicated, may hold values from 0 to 15, each once
- panel_first: float32 [2, 8192, 512], P(None, 'row'), may hold values from -0.1875 to 0.1875
- panel_second: float32 [2, 8192, 512], P(None, 'row'), may hold values from -0.1875 to 0.1875
- inverse_first: float32 [2, 512, 512], replicated, may hold values from -0.1875 to 0.1875
- inverse_second: float32 [2, 512, 512], replicated, may hold values from -0.1875 to 0.1875
Outputs:
- solved_rhs: float32 [2, 128, 8192], P(None, 'rhs', 'row')
The draws below stay inside these ranges and needn't reach their ends.
Inputs may be any that keep to these rules, and one draw needn't show every extreme that they name: `pivots`: each row number occurs once. `owners`: each device index along row occurs once.
All inputs are finite; a program needn't handle non-finite values.
Results may differ from the reference program's by a relative error of at most 0.0001.
Values sent between devices are 32-bit elements; how exact they have to be, the bound alone decides.
A program may use at most 128 MiB of HBM per device.

```python
import jax
import jax.numpy as jnp
from jax import lax

BLK = 512
NRHS = 128
ROWS = 8192
N_ROW = 16


def block_levels(stream_key, extent, split, low, high):
    gain = 1.0
    for position, shards_of in split:
        steps = jax.random.uniform(jax.random.fold_in(jax.random.fold_in(stream_key, 6), position), (shards_of,), jnp.float32, low / len(split), high / len(split))
        gain = gain * jnp.repeat(jnp.exp(steps), extent[position] // shards_of).reshape((-1,) + (1,) * (len(extent) - 1 - position))
    return gain


def normal_values(stream_key, dims, width, most, pieces=(), held_as=jnp.bfloat16):
    result = jax.random.normal(stream_key, dims, jnp.float32) * width
    if len(pieces) > 0:
        result = block_levels(stream_key, dims, pieces, -0.22, 0.18) * result
    return jnp.clip(result, min=-most, max=most).astype(held_as)


def setup_inputs(seed: int = 0) -> dict:
    arg_keys = jax.random.split(jax.random.key(seed), 8)
    return {
        "rhs_in": normal_values(arg_keys[0], (2, NRHS, ROWS), 1.0, 6.0, ((1, 32),), jnp.float32),
        "pivots": jax.random.permutation(arg_keys[1], ROWS).astype(jnp.int32),
        "owners": jax.random.permutation(arg_keys[2], N_ROW).astype(jnp.int32),
        "panel_first": normal_values(arg_keys[3], (2, ROWS, BLK), (2 * BLK) ** -0.5, 0.1875, ((1, 16),), jnp.float32),
        "panel_second": normal_values(arg_keys[4], (2, ROWS, BLK), (2 * BLK) ** -0.5, 0.1875, ((1, 16),), jnp.float32),
        "inverse_first": normal_values(arg_keys[5], (2, BLK, BLK), (2 * BLK) ** -0.5, 0.1875, (), jnp.float32),
        "inverse_second": normal_values(arg_keys[6], (2, BLK, BLK), (2 * BLK) ** -0.5, 0.1875, (), jnp.float32),
    }


def complex_product(operand, matrix):
    contract = (((1,), (1,)), ((), ()))

    def multiply(first, second):
        return lax.dot_general(first, second, contract, precision=lax.Precision.HIGHEST, preferred_element_type=jnp.float32)

    real_part = multiply(operand[0], matrix[0]) - multiply(operand[1], matrix[1])
    imag_part = multiply(operand[0], matrix[1]) + multiply(operand[1], matrix[0])
    return jnp.stack([real_part, imag_part])


def reference(rhs_in, pivots, owners, panel_first, panel_second, inverse_first, inverse_second):
    blocks = owners.shape[0]
    slot_block = jnp.zeros((blocks,), jnp.int32).at[owners].set(jnp.arange(blocks, dtype=jnp.int32))
    row_index = (slot_block[:, None] * BLK + jnp.arange(BLK, dtype=jnp.int32)[None, :]).reshape(-1)
    current = jnp.take(rhs_in, jnp.take(pivots, row_index), axis=2)
    row_block = jnp.repeat(slot_block, BLK)
    sections = ((panel_first, inverse_first), (panel_second, inverse_second))
    for block_step in range(2):
        panel_rows, inverse = sections[block_step]
        holder = (owners[block_step] * BLK).astype(jnp.int32)
        rhs_block = lax.dynamic_slice_in_dim(current, holder, BLK, 2)
        solution = complex_product(rhs_block, inverse)
        update = complex_product(solution, panel_rows)
        later = (row_block > block_step)[None, None, :]
        current = jnp.where(later, current - update, current)
        current = lax.dynamic_update_slice_in_dim(current, solution, holder, 2)
    return current
```

```python
import functools

import jax
import jax.numpy as jnp
from jax import lax
from jax.experimental import pallas as pl
from jax.experimental.pallas import tpu as pltpu
from jax.sharding import PartitionSpec as P

LANES = 128
MESH = pl.DeviceIdType.MESH


def split_matrix(matrix, high, low):
    depth = matrix.shape[2]
    for part in range(2):
        columns = slice(part * depth, (part + 1) * depth)
        values = matrix[part]
        rounded = values.astype(jnp.bfloat16)
        high[:, columns] = rounded
        low[:, columns] = (values - rounded.astype(jnp.float32)).astype(jnp.bfloat16)


def complex_product(operand, high, low):
    groups, size, depth = operand.shape
    half = size // 2
    swapped = pltpu.roll(operand, half, axis=1)
    is_real = lax.broadcasted_iota(jnp.int32, operand.shape, 1) < half
    swapped = jnp.where(is_real, -swapped, swapped)
    rows = groups * size
    wide = jnp.concatenate(
        [operand.reshape(rows, depth), swapped.reshape(rows, depth)], axis=1
    )
    top = wide.astype(jnp.bfloat16).astype(jnp.float32)
    both = jnp.concatenate([top, wide - top], axis=0).astype(jnp.bfloat16)
    contract = (((1,), (1,)), ((), ()))
    main = lax.dot_general(both, high[...], contract, preferred_element_type=jnp.float32)
    first = both[:rows] if rows % 16 == 0 else both
    rest = lax.dot_general(first, low[...], contract, preferred_element_type=jnp.float32)
    return (main[:rows] + main[rows:] + rest[:rows]).reshape(groups, size, depth)


def kernel(
    axis,
    count,
    owners,
    pivots,
    rhs_in,
    panel_first,
    panel_second,
    inverse_first,
    inverse_second,
    out,
    raw,
    values,
    permuted,
    current,
    updated,
    returned,
    solution_zero,
    solution_one,
    factors,
    high,
    low,
    load_sem,
    send_sem,
    receive_sem,
):
    me = lax.axis_index(axis)
    half = raw.shape[1]
    length = raw.shape[2]
    block_size = permuted.shape[2]
    tiles = block_size // LANES

    loads = [pltpu.make_async_copy(rhs_in, raw, load_sem.at[4])]
    for place, source in enumerate((inverse_first, panel_first, inverse_second, panel_second)):
        loads.append(pltpu.make_async_copy(source, factors.at[place], load_sem.at[place]))
    for load in loads:
        load.start()

    def partner(step):
        return lax.rem(me + step, count)

    barrier = pltpu.get_barrier_semaphore()

    @pl.loop(1, count)
    def _(step):
        pl.semaphore_signal(
            barrier, inc=1, device_id={axis: partner(step)}, device_id_type=MESH
        )

    def remote(phase, source, target, peer, slot):
        return pltpu.make_async_remote_copy(
            src_ref=source,
            dst_ref=target,
            send_sem=send_sem.at[phase, peer],
            recv_sem=receive_sem.at[phase, slot],
            device_id={axis: peer},
            device_id_type=MESH,
        )

    def finish_receives(phase, target):
        @pl.loop(1, count)
        def _(step):
            peer = partner(step)
            remote(phase, target.at[peer], target.at[peer], peer, peer).wait_recv()

    def block_at(slot):
        block = jnp.int32(0)
        for j in range(count):
            block = jnp.where(owners[j] == slot, j, block)
        return block

    def gather(block, store):
        index = [pivots[pl.ds(block * tiles + t, 1), :] for t in range(tiles)]
        index = [jnp.broadcast_to(row, (2 * half, LANES)) for row in index]
        lane = [row % LANES for row in index]
        group = [row // LANES for row in index]
        taken = [jnp.zeros((2 * half, LANES), jnp.float32) for _ in range(tiles)]
        for h in range(length // LANES):
            source = values[:, h * LANES : (h + 1) * LANES]
            for t in range(tiles):
                picked = jnp.take_along_axis(source, lane[t], axis=1)
                taken[t] = jnp.where(group[t] == h, picked, taken[t])
        store(jnp.concatenate(taken, axis=1))

    def prepare(place):
        loads[place + 1].wait()
        split_matrix(factors.at[place], high.at[place], low.at[place])

    prepare(0)
    loads[0].wait()
    values[...] = jnp.concatenate([raw[0], raw[1]], axis=0)

    def solve_zero(leading):
        solution_zero[me] = complex_product(leading[None], high.at[0], low.at[0])[0]

    gather(0, solve_zero)
    pl.semaphore_wait(barrier, count - 1)

    @pl.loop(1, count)
    def _(step):
        peer = partner(step)
        remote(0, solution_zero.at[me], solution_zero.at[me], peer, me).start()

    @pl.loop(1, count)
    def _(step):
        peer = partner(step)

        def store(chunk):
            permuted[peer] = chunk

        gather(block_at(peer), store)
        remote(1, permuted.at[peer], current.at[me], peer, me).start()

    my_block = block_at(me)

    def store_own(chunk):
        current[me] = chunk

    gather(my_block, store_own)
    prepare(1)
    prepare(2)
    prepare(3)

    finish_receives(0, solution_zero)
    finish_receives(1, current)
    zero = solution_zero[...]
    before = current[...]
    block = jnp.full(before.shape, my_block, jnp.int32)
    after = before - complex_product(zero, high.at[1], low.at[1])
    after = jnp.where(block > 0, after, zero)
    updated[...] = after
    returned[me] = updated[me]

    @pl.loop(1, count)
    def _(step):
        peer = partner(step)
        remote(2, updated.at[peer], returned.at[me], peer, me).start()

    finish_receives(2, returned)
    second = returned[owners[1]]
    solution_one[me] = complex_product(second[None], high.at[2], low.at[2])[0]

    @pl.loop(1, count)
    def _(step):
        peer = partner(step)
        remote(3, solution_one.at[me], solution_one.at[me], peer, me).start()

    finish_receives(3, solution_one)
    one = solution_one[...]
    before = updated[...]
    after = before - complex_product(one, high.at[3], low.at[3])
    after = jnp.where(block > 1, after, jnp.where(block == 1, one, before))
    for part in range(2):
        rows = after[:, part * half : (part + 1) * half, :]
        out[part] = rows.reshape(count * half, block_size)

    @pl.loop(1, count)
    def _(step):
        peer = partner(step)
        remote(0, solution_zero.at[me], solution_zero.at[me], peer, me).wait_send()
        remote(1, permuted.at[peer], current.at[me], peer, me).wait_send()
        remote(2, updated.at[peer], returned.at[me], peer, me).wait_send()
        remote(3, solution_one.at[me], solution_one.at[me], peer, me).wait_send()


def shards(rhs_in, pivots, owners, panel_first, panel_second, inverse_first, inverse_second, *, count):
    parts, half, length = rhs_in.shape
    block_size = panel_first.shape[2]
    chunks = (count, parts * half, block_size)
    vmem = pl.BlockSpec(memory_space=pltpu.VMEM)
    anywhere = pl.BlockSpec(memory_space=pl.ANY)
    return pl.pallas_call(
        functools.partial(kernel, "row", count),
        out_shape=jax.ShapeDtypeStruct((parts, count * half, block_size), jnp.float32),
        in_specs=[pl.BlockSpec(memory_space=pltpu.SMEM), vmem] + [anywhere] * 5,
        out_specs=vmem,
        scratch_shapes=[
            pltpu.VMEM((parts, half, length), jnp.float32),
            pltpu.VMEM((parts * half, length), jnp.float32),
            pltpu.VMEM(chunks, jnp.float32),
            pltpu.VMEM(chunks, jnp.float32),
            pltpu.VMEM(chunks, jnp.float32),
            pltpu.VMEM(chunks, jnp.float32),
            pltpu.VMEM(chunks, jnp.float32),
            pltpu.VMEM(chunks, jnp.float32),
            pltpu.VMEM((4, parts, block_size, block_size), jnp.float32),
            pltpu.VMEM((4, block_size, parts * block_size), jnp.bfloat16),
            pltpu.VMEM((4, block_size, parts * block_size), jnp.bfloat16),
            pltpu.SemaphoreType.DMA((5,)),
            pltpu.SemaphoreType.DMA((4, count)),
            pltpu.SemaphoreType.DMA((4, count)),
        ],
        compiler_params=pltpu.CompilerParams(
            collective_id=0, has_side_effects=True, vmem_limit_bytes=48 * 1024 * 1024
        ),
        cost_estimate=pl.CostEstimate(flops=4 * 10**9, bytes_accessed=9 * 10**6, transcendentals=0),
    )(
        owners,
        pivots.reshape(length // LANES, LANES),
        rhs_in,
        panel_first,
        panel_second,
        inverse_first,
        inverse_second,
    )


def solution(mesh):
    return jax.shard_map(
        functools.partial(shards, count=mesh.shape["row"]),
        mesh=mesh,
        in_specs=(
            P(None, ("rhs", "row"), None),
            P(),
            P(),
            P(None, "row", None),
            P(None, "row", None),
            P(),
            P(),
        ),
        out_specs=P(None, "rhs", "row"),
        check_vma=False,
    )
```

```python
import functools

import jax
import jax.numpy as jnp
from jax import lax
from jax.experimental import pallas as pl
from jax.experimental.pallas import tpu as pltpu
from jax.sharding import PartitionSpec as P

LANES = 128
MESH = pl.DeviceIdType.MESH


def split_matrix(matrix, high, low):
    depth = matrix.shape[2]
    for part in range(2):
        columns = slice(part * depth, (part + 1) * depth)
        values = matrix[part]
        rounded = values.astype(jnp.bfloat16)
        high[:, columns] = rounded
        low[:, columns] = (values - rounded.astype(jnp.float32)).astype(jnp.bfloat16)


def complex_product(operand, high, low):
    groups, size, depth = operand.shape
    half = size // 2
    swapped = pltpu.roll(operand, half, axis=1)
    is_real = lax.broadcasted_iota(jnp.int32, operand.shape, 1) < half
    swapped = jnp.where(is_real, -swapped, swapped)
    rows = groups * size
    wide = jnp.concatenate(
        [operand.reshape(rows, depth), swapped.reshape(rows, depth)], axis=1
    )
    top = wide.astype(jnp.bfloat16).astype(jnp.float32)
    both = jnp.concatenate([top, wide - top], axis=0).astype(jnp.bfloat16)
    contract = (((1,), (1,)), ((), ()))
    main = lax.dot_general(both, high[...], contract, preferred_element_type=jnp.float32)
    first = both[:rows] if rows % 16 == 0 else both
    rest = lax.dot_general(first, low[...], contract, preferred_element_type=jnp.float32)
    return (main[:rows] + main[rows:] + rest[:rows]).reshape(groups, size, depth)


def kernel(
    axis,
    count,
    owners,
    pivots,
    rhs_in,
    panel_first,
    panel_second,
    inverse_first,
    inverse_second,
    out,
    raw,
    values,
    permuted,
    current,
    updated,
    merged,
    from_sibling,
    returned,
    solution_zero,
    solution_one,
    factors,
    high,
    low,
    load_sem,
    send_sem,
    receive_sem,
):
    me = lax.axis_index(axis)
    half = raw.shape[1]
    length = raw.shape[2]
    block_size = permuted.shape[2]
    tiles = block_size // LANES
    pairs = count // 2
    chip = lax.div(me, 2)
    core = lax.rem(me, 2)
    sibling = me + 1 - 2 * core
    middle = pairs // 2
    side = lax.div(chip, middle)
    own_slot = core * pairs + chip

    loads = [pltpu.make_async_copy(rhs_in, raw, load_sem.at[4])]
    for place, source in enumerate((inverse_first, panel_first, inverse_second, panel_second)):
        loads.append(pltpu.make_async_copy(source, factors.at[place], load_sem.at[place]))
    for load in loads:
        load.start()

    def each_chip(body):
        @pl.loop(0, middle)
        def _(step):
            body((1 - side) * middle + lax.rem(chip + step, middle))

        @pl.loop(1, middle)
        def _(step):
            body(side * middle + lax.rem(chip + step, middle))

    def each_chip_near_first(body):
        @pl.loop(1, middle)
        def _(step):
            body(side * middle + lax.rem(chip + step, middle))

        @pl.loop(0, middle)
        def _(step):
            body((1 - side) * middle + lax.rem(chip + step, middle))

    barrier = pltpu.get_barrier_semaphore()

    @pl.loop(1, count)
    def _(step):
        pl.semaphore_signal(
            barrier,
            inc=1,
            device_id={axis: lax.rem(me + step, count)},
            device_id_type=MESH,
        )

    def remote(phase, source, target, peer, send_slot, receive_slot):
        return pltpu.make_async_remote_copy(
            src_ref=source,
            dst_ref=target,
            send_sem=send_sem.at[phase, send_slot],
            recv_sem=receive_sem.at[phase, receive_slot],
            device_id={axis: peer},
            device_id_type=MESH,
        )

    def spread(phase, chunks):
        def direct(other):
            return remote(
                phase, chunks.at[own_slot], chunks.at[own_slot], 2 * other + core, other, own_slot
            )

        def relay(other):
            slot = core * pairs + other
            return remote(phase, chunks.at[slot], chunks.at[slot], sibling, pairs + other, slot)

        def begin():
            each_chip(lambda other: direct(other).start())
            relay(chip).start()

        def forward():
            def one(other):
                slot = core * pairs + other
                remote(
                    phase, chunks.at[slot], chunks.at[slot], 2 * other + core, other, slot
                ).wait_recv()
                relay(other).start()

            each_chip_near_first(one)

        def complete():
            @pl.loop(0, pairs)
            def _(other):
                slot = (1 - core) * pairs + other
                remote(
                    phase, chunks.at[slot], chunks.at[slot], sibling, pairs + other, slot
                ).wait_recv()

        def drain():
            each_chip(lambda other: direct(other).wait_send())

            @pl.loop(0, pairs)
            def _(other):
                relay(other).wait_send()

        return begin, forward, complete, drain

    def deal(target_chip, target_core):
        slot = target_core * pairs + target_chip
        return remote(
            2,
            permuted.at[slot],
            current.at[own_slot],
            2 * target_chip + target_core,
            slot,
            own_slot,
        )

    def hand_back(other):
        return remote(
            3, merged.at[other], returned.at[chip], 2 * other + core, other, chip
        )

    def pair_copy():
        return remote(
            3,
            updated.at[pl.ds((1 - core) * pairs, pairs)],
            from_sibling,
            sibling,
            pairs,
            pairs,
        )

    def block_at(slot):
        block = jnp.int32(0)
        for j in range(count):
            block = jnp.where(owners[j] == slot, j, block)
        return block

    def gather(block, store):
        index = [pivots[pl.ds(block * tiles + t, 1), :] for t in range(tiles)]
        index = [jnp.broadcast_to(row, (2 * half, LANES)) for row in index]
        lane = [row % LANES for row in index]
        group = [row // LANES for row in index]
        taken = [jnp.zeros((2 * half, LANES), jnp.float32) for _ in range(tiles)]
        for h in range(length // LANES):
            source = values[:, h * LANES : (h + 1) * LANES]
            for t in range(tiles):
                picked = jnp.take_along_axis(source, lane[t], axis=1)
                taken[t] = jnp.where(group[t] == h, picked, taken[t])
        store(jnp.concatenate(taken, axis=1))

    def prepare(place):
        loads[place + 1].wait()
        split_matrix(factors.at[place], high.at[place], low.at[place])

    def deal_one(target_chip, target_core):
        def store(chunk):
            permuted[target_core * pairs + target_chip] = chunk

        gather(block_at(2 * target_chip + target_core), store)
        deal(target_chip, target_core).start()

    begin_zero, forward_zero, complete_zero, drain_zero = spread(0, solution_zero)
    begin_one, forward_one, complete_one, drain_one = spread(1, solution_one)

    loads[0].wait()
    values[...] = jnp.concatenate([raw[0], raw[1]], axis=0)
    pl.semaphore_wait(barrier, count - 1)

    @pl.loop(0, middle)
    def _(step):
        deal_one((1 - side) * middle + lax.rem(chip + step, middle), core)

    prepare(0)

    def solve_zero(leading):
        solution_zero[own_slot] = complex_product(leading[None], high.at[0], low.at[0])[0]

    gather(0, solve_zero)
    begin_zero()

    @pl.loop(0, middle)
    def _(step):
        deal_one((1 - side) * middle + lax.rem(chip + step, middle), 1 - core)

    @pl.loop(1, 2 * middle)
    def _(step):
        deal_one(
            side * middle + lax.rem(chip + lax.div(step, 2), middle),
            lax.rem(core + step, 2),
        )

    my_block = block_at(me)

    def store_own(chunk):
        current[own_slot] = chunk

    gather(my_block, store_own)
    forward_zero()
    prepare(1)
    complete_zero()
    updated[...] = complex_product(solution_zero[...], high.at[1], low.at[1])

    @pl.loop(1, count)
    def _(step):
        slot = lax.rem(own_slot + step, count)
        remote(2, current.at[slot], current.at[slot], sibling, slot, slot).wait_recv()

    def update_half(first):
        rows = pl.ds(first, pairs)
        before = current[rows]
        block = jnp.full(before.shape, my_block, jnp.int32)
        updated[rows] = jnp.where(block > 0, before - updated[rows], solution_zero[rows])

    update_half((1 - core) * pairs)
    pair_copy().start()
    update_half(core * pairs)
    prepare(2)
    pair_copy().wait_recv()
    mine = updated[pl.ds(core * pairs, pairs)]
    theirs = jnp.full(mine.shape, block_at(sibling), jnp.int32) == 1
    merged[...] = jnp.where(theirs, from_sibling[...], mine)
    each_chip(lambda other: hand_back(other).start())
    returned[chip] = merged[chip]
    prepare(3)

    @pl.loop(1, pairs)
    def _(step):
        other = lax.rem(chip + step, pairs)
        remote(3, returned.at[other], returned.at[other], sibling, other, other).wait_recv()

    second = returned[lax.div(owners[1], 2)]
    solution_one[own_slot] = complex_product(second[None], high.at[2], low.at[2])[0]
    begin_one()
    forward_one()

    def last_half(first):
        rows = pl.ds(first, pairs)
        one = solution_one[rows]
        before = updated[rows]
        block = jnp.full(before.shape, my_block, jnp.int32)
        after = before - complex_product(one, high.at[3], low.at[3])
        current[rows] = jnp.where(block > 1, after, jnp.where(block == 1, one, before))

    last_half(core * pairs)
    complete_one()
    last_half((1 - core) * pairs)
    for part in range(2):
        rows = slice(part * half, (part + 1) * half)
        both = [current[c * pairs : (c + 1) * pairs, rows, :] for c in range(2)]
        out[part] = jnp.concatenate(both, axis=1).reshape(count * half, block_size)

    drain_zero()
    drain_one()
    pair_copy().wait_send()
    each_chip(lambda other: hand_back(other).wait_send())

    @pl.loop(1, count)
    def _(step):
        slot = lax.rem(own_slot + step, count)
        deal(lax.rem(slot, pairs), lax.div(slot, pairs)).wait_send()


def shards(rhs_in, pivots, owners, panel_first, panel_second, inverse_first, inverse_second, *, count):
    parts, half, length = rhs_in.shape
    block_size = panel_first.shape[2]
    chunks = (count, parts * half, block_size)
    part_chunks = (count // 2, parts * half, block_size)
    vmem = pl.BlockSpec(memory_space=pltpu.VMEM)
    anywhere = pl.BlockSpec(memory_space=pl.ANY)
    return pl.pallas_call(
        functools.partial(kernel, "row", count),
        out_shape=jax.ShapeDtypeStruct((parts, count * half, block_size), jnp.float32),
        in_specs=[pl.BlockSpec(memory_space=pltpu.SMEM), vmem] + [anywhere] * 5,
        out_specs=vmem,
        scratch_shapes=[
            pltpu.VMEM((parts, half, length), jnp.float32),
            pltpu.VMEM((parts * half, length), jnp.float32),
            pltpu.VMEM(chunks, jnp.float32),
            pltpu.VMEM(chunks, jnp.float32),
            pltpu.VMEM(chunks, jnp.float32),
            pltpu.VMEM(part_chunks, jnp.float32),
            pltpu.VMEM(part_chunks, jnp.float32),
            pltpu.VMEM(part_chunks, jnp.float32),
            pltpu.VMEM(chunks, jnp.float32),
            pltpu.VMEM(chunks, jnp.float32),
            pltpu.VMEM((4, parts, block_size, block_size), jnp.float32),
            pltpu.VMEM((4, block_size, parts * block_size), jnp.bfloat16),
            pltpu.VMEM((4, block_size, parts * block_size), jnp.bfloat16),
            pltpu.SemaphoreType.DMA((5,)),
            pltpu.SemaphoreType.DMA((4, count)),
            pltpu.SemaphoreType.DMA((4, count)),
        ],
        compiler_params=pltpu.CompilerParams(
            collective_id=0, has_side_effects=True, vmem_limit_bytes=62 * 1024 * 1024
        ),
        cost_estimate=pl.CostEstimate(flops=4 * 10**9, bytes_accessed=9 * 10**6, transcendentals=0),
    )(
        owners,
        pivots.reshape(length // LANES, LANES),
        rhs_in,
        panel_first,
        panel_second,
        inverse_first,
        inverse_second,
    )


def solution(mesh):
    return jax.shard_map(
        functools.partial(shards, count=mesh.shape["row"]),
        mesh=mesh,
        in_specs=(
            P(None, ("rhs", "row"), None),
            P(),
            P(),
            P(None, "row", None),
            P(None, "row", None),
            P(),
            P(),
        ),
        out_specs=P(None, "rhs", "row"),
        check_vma=False,
    )
```

```python
import functools

import jax
import jax.numpy as jnp
from jax import lax
from jax.experimental import pallas as pl
from jax.experimental.pallas import tpu as pltpu
from jax.sharding import PartitionSpec as P

LANES = 128
SHIFT = 8
WIDTH = 1 << SHIFT
MESH = pl.DeviceIdType.MESH


def split_matrix(matrix, high, low):
    depth = matrix.shape[2]
    for part in range(2):
        columns = slice(part * depth, (part + 1) * depth)
        values = matrix[part]
        rounded = values.astype(jnp.bfloat16)
        high[:, columns] = rounded
        low[:, columns] = (values - rounded.astype(jnp.float32)).astype(jnp.bfloat16)


def complex_product(operand, high, low):
    groups, size, depth = operand.shape
    half = size // 2
    swapped = pltpu.roll(operand, half, axis=1)
    is_real = lax.broadcasted_iota(jnp.int32, operand.shape, 1) < half
    swapped = jnp.where(is_real, -swapped, swapped)
    rows = groups * size
    wide = jnp.concatenate(
        [operand.reshape(rows, depth), swapped.reshape(rows, depth)], axis=1
    )
    top = wide.astype(jnp.bfloat16).astype(jnp.float32)
    both = jnp.concatenate([top, wide - top], axis=0).astype(jnp.bfloat16)
    contract = (((1,), (1,)), ((), ()))
    main = lax.dot_general(both, high[...], contract, preferred_element_type=jnp.float32)
    first = both[:rows] if rows % 16 == 0 else both
    rest = lax.dot_general(first, low[...], contract, preferred_element_type=jnp.float32)
    return (main[:rows] + main[rows:] + rest[:rows]).reshape(groups, size, depth)


def kernel(
    axis,
    count,
    owners_in,
    pivots_in,
    rhs_in,
    panel_first,
    panel_second,
    inverse_first,
    inverse_second,
    out,
    owners,
    pivots,
    raw,
    values,
    table,
    permuted,
    current,
    updated,
    merged,
    from_sibling,
    returned,
    solution_zero,
    solution_one,
    factors,
    high,
    low,
    load_sem,
    send_sem,
    receive_sem,
):
    me = lax.axis_index(axis)
    half = raw.shape[1]
    length = raw.shape[2]
    block_size = permuted.shape[2]
    tiles = block_size // LANES
    pairs = count // 2
    chip = lax.div(me, 2)
    core = lax.rem(me, 2)
    sibling = me + 1 - 2 * core
    middle = pairs // 2
    side = lax.div(chip, middle)
    own_slot = core * pairs + chip

    loads = [pltpu.make_async_copy(rhs_in, raw, load_sem.at[4])]
    for place, source in enumerate((inverse_first, panel_first, inverse_second, panel_second)):
        loads.append(pltpu.make_async_copy(source, factors.at[place], load_sem.at[place]))
    small = [
        pltpu.make_async_copy(owners_in, owners, load_sem.at[5]),
        pltpu.make_async_copy(pivots_in, pivots, load_sem.at[6]),
    ]
    for load in small + loads:
        load.start()

    def each_chip(body):
        @pl.loop(0, middle)
        def _(step):
            body((1 - side) * middle + lax.rem(chip + step, middle))

        @pl.loop(1, middle)
        def _(step):
            body(side * middle + lax.rem(chip + step, middle))

    def each_chip_near_first(body):
        @pl.loop(1, middle)
        def _(step):
            body(side * middle + lax.rem(chip + step, middle))

        @pl.loop(0, middle)
        def _(step):
            body((1 - side) * middle + lax.rem(chip + step, middle))

    barrier = pltpu.get_barrier_semaphore()

    @pl.loop(1, count)
    def _(step):
        pl.semaphore_signal(
            barrier,
            inc=1,
            device_id={axis: lax.rem(me + step, count)},
            device_id_type=MESH,
        )

    def remote(phase, source, target, peer, send_slot, receive_slot):
        return pltpu.make_async_remote_copy(
            src_ref=source,
            dst_ref=target,
            send_sem=send_sem.at[phase, send_slot],
            recv_sem=receive_sem.at[phase, receive_slot],
            device_id={axis: peer},
            device_id_type=MESH,
        )

    def spread(phase, chunks):
        def direct(other):
            return remote(
                phase, chunks.at[own_slot], chunks.at[own_slot], 2 * other + core, other, own_slot
            )

        def relay(other):
            slot = core * pairs + other
            return remote(phase, chunks.at[slot], chunks.at[slot], sibling, pairs + other, slot)

        def begin():
            each_chip(lambda other: direct(other).start())
            relay(chip).start()

        def forward():
            def one(other):
                slot = core * pairs + other
                remote(
                    phase, chunks.at[slot], chunks.at[slot], 2 * other + core, other, slot
                ).wait_recv()
                relay(other).start()

            each_chip_near_first(one)

        def complete():
            @pl.loop(0, pairs)
            def _(other):
                slot = (1 - core) * pairs + other
                remote(
                    phase, chunks.at[slot], chunks.at[slot], sibling, pairs + other, slot
                ).wait_recv()

        def drain():
            each_chip(lambda other: direct(other).wait_send())

            @pl.loop(0, pairs)
            def _(other):
                relay(other).wait_send()

        return begin, forward, complete, drain

    def deal(target_chip, target_core):
        slot = target_core * pairs + target_chip
        return remote(
            2,
            permuted.at[slot],
            current.at[own_slot],
            2 * target_chip + target_core,
            slot,
            own_slot,
        )

    def hand_back(other):
        return remote(
            3, merged.at[other], returned.at[chip], 2 * other + core, other, chip
        )

    def pair_copy():
        return remote(
            3,
            updated.at[pl.ds((1 - core) * pairs, pairs)],
            from_sibling,
            sibling,
            pairs,
            pairs,
        )

    def block_at(slot):
        block = jnp.int32(0)
        for j in range(count):
            block = jnp.where(owners[j] == slot, j, block)
        return block

    def gather(block):
        groups = length // WIDTH
        index = [pivots[pl.ds(block * tiles + t, 1), :] for t in range(tiles)]
        index = jnp.concatenate(index, axis=1)
        column = jnp.broadcast_to(index & (WIDTH - 1), (WIDTH, block_size))
        place = lax.broadcasted_iota(jnp.int32, (WIDTH, block_size), 0)
        chosen = jnp.where(column == place, 1.0, 0.0).astype(jnp.bfloat16)
        found = jnp.dot(table[...], chosen, preferred_element_type=jnp.float32)
        group = jnp.broadcast_to(lax.shift_right_logical(index, SHIFT), (2 * half, block_size))
        taken = jnp.zeros((2 * half, block_size), jnp.float32)
        for g in range(groups):
            top = found[g * 2 * half : (g + 1) * 2 * half]
            rest = found[(groups + g) * 2 * half : (groups + g + 1) * 2 * half]
            taken = jnp.where(group == g, top + rest, taken)
        return taken

    def prepare(place):
        loads[place + 1].wait()
        split_matrix(factors.at[place], high.at[place], low.at[place])

    def gather_pair(target_chip):
        for target_core in range(2):
            chunk = gather(block_at(2 * target_chip + target_core))
            permuted[target_core * pairs + target_chip] = chunk

    def deal_chip(step):
        near = lax.div(step, middle)
        target_side = (1 - side) * (1 - near) + side * near
        target_chip = target_side * middle + lax.rem(chip + 1 + step, middle)
        gather_pair(target_chip)
        for target_core in range(2):
            deal(target_chip, target_core).start()

    begin_zero, forward_zero, complete_zero, drain_zero = spread(0, solution_zero)
    begin_one, forward_one, complete_one, drain_one = spread(1, solution_one)

    for load in small:
        load.wait()
    loads[0].wait()
    groups = length // WIDTH
    for g in range(groups):
        columns = slice(g * WIDTH, (g + 1) * WIDTH)
        wide = jnp.concatenate([raw[0, :, columns], raw[1, :, columns]], axis=0)
        values[g * 2 * half : (g + 1) * 2 * half, :] = wide
    rounded = values[...].astype(jnp.bfloat16)
    rows = groups * 2 * half
    table[:rows] = rounded
    table[rows:] = (values[...] - rounded.astype(jnp.float32)).astype(jnp.bfloat16)
    pl.semaphore_wait(barrier, count - 1)

    @pl.loop(0, middle // 2)
    def _(step):
        deal_chip(step)

    prepare(0)
    solution_zero[own_slot] = complex_product(gather(0)[None], high.at[0], low.at[0])[0]
    begin_zero()

    @pl.loop(middle // 2, pairs - 1)
    def _(step):
        deal_chip(step)

    my_block = block_at(me)
    gather_pair(chip)
    deal(chip, 1 - core).start()
    current[own_slot] = permuted[own_slot]
    forward_zero()
    prepare(1)
    complete_zero()
    updated[...] = complex_product(solution_zero[...], high.at[1], low.at[1])

    @pl.loop(1, count)
    def _(step):
        slot = lax.rem(own_slot + step, count)
        remote(2, current.at[slot], current.at[slot], sibling, slot, slot).wait_recv()

    def update_half(first):
        rows = pl.ds(first, pairs)
        before = current[rows]
        block = jnp.full(before.shape, my_block, jnp.int32)
        updated[rows] = jnp.where(block > 0, before - updated[rows], solution_zero[rows])

    update_half((1 - core) * pairs)
    pair_copy().start()
    update_half(core * pairs)
    prepare(2)
    pair_copy().wait_recv()
    mine = updated[pl.ds(core * pairs, pairs)]
    theirs = jnp.full(mine.shape, block_at(sibling), jnp.int32) == 1
    merged[...] = jnp.where(theirs, from_sibling[...], mine)
    each_chip(lambda other: hand_back(other).start())
    returned[chip] = merged[chip]
    prepare(3)

    @pl.loop(1, pairs)
    def _(step):
        other = lax.rem(chip + step, pairs)
        remote(3, returned.at[other], returned.at[other], sibling, other, other).wait_recv()

    second = returned[lax.div(owners[1], 2)]
    solution_one[own_slot] = complex_product(second[None], high.at[2], low.at[2])[0]
    begin_one()
    forward_one()

    def last_half(first):
        rows = pl.ds(first, pairs)
        one = solution_one[rows]
        before = updated[rows]
        block = jnp.full(before.shape, my_block, jnp.int32)
        after = before - complex_product(one, high.at[3], low.at[3])
        current[rows] = jnp.where(block > 1, after, jnp.where(block == 1, one, before))

    last_half(core * pairs)
    complete_one()
    last_half((1 - core) * pairs)
    for part in range(2):
        rows = slice(part * half, (part + 1) * half)
        both = [current[c * pairs : (c + 1) * pairs, rows, :] for c in range(2)]
        out[part] = jnp.concatenate(both, axis=1).reshape(count * half, block_size)

    drain_zero()
    drain_one()
    pair_copy().wait_send()
    each_chip(lambda other: hand_back(other).wait_send())

    @pl.loop(1, count)
    def _(step):
        slot = lax.rem(own_slot + step, count)
        deal(lax.rem(slot, pairs), lax.div(slot, pairs)).wait_send()


def shards(rhs_in, pivots, owners, panel_first, panel_second, inverse_first, inverse_second, *, count):
    parts, half, length = rhs_in.shape
    block_size = panel_first.shape[2]
    chunks = (count, parts * half, block_size)
    part_chunks = (count // 2, parts * half, block_size)
    return pl.pallas_call(
        functools.partial(kernel, "row", count),
        out_shape=jax.ShapeDtypeStruct((parts, count * half, block_size), jnp.float32),
        in_specs=[pl.BlockSpec(memory_space=pltpu.HBM)] * 7,
        out_specs=pl.BlockSpec(memory_space=pltpu.VMEM),
        scratch_shapes=[
            pltpu.SMEM((count,), jnp.int32),
            pltpu.VMEM((length // LANES, LANES), jnp.int32),
            pltpu.VMEM((parts, half, length), jnp.float32),
            pltpu.VMEM((parts * half * length // WIDTH, WIDTH), jnp.float32),
            pltpu.VMEM((2 * parts * half * length // WIDTH, WIDTH), jnp.bfloat16),
            pltpu.VMEM(chunks, jnp.float32),
            pltpu.VMEM(chunks, jnp.float32),
            pltpu.VMEM(chunks, jnp.float32),
            pltpu.VMEM(part_chunks, jnp.float32),
            pltpu.VMEM(part_chunks, jnp.float32),
            pltpu.VMEM(part_chunks, jnp.float32),
            pltpu.VMEM(chunks, jnp.float32),
            pltpu.VMEM(chunks, jnp.float32),
            pltpu.VMEM((4, parts, block_size, block_size), jnp.float32),
            pltpu.VMEM((4, block_size, parts * block_size), jnp.bfloat16),
            pltpu.VMEM((4, block_size, parts * block_size), jnp.bfloat16),
            pltpu.SemaphoreType.DMA((7,)),
            pltpu.SemaphoreType.DMA((4, count)),
            pltpu.SemaphoreType.DMA((4, count)),
        ],
        compiler_params=pltpu.CompilerParams(
            collective_id=0, has_side_effects=True, vmem_limit_bytes=57 * 1024 * 1024
        ),
        cost_estimate=pl.CostEstimate(flops=4 * 10**9, bytes_accessed=9 * 10**6, transcendentals=0),
    )(
        owners,
        pivots.reshape(length // LANES, LANES),
        rhs_in,
        panel_first,
        panel_second,
        inverse_first,
        inverse_second,
    )


def solution(mesh):
    return jax.shard_map(
        functools.partial(shards, count=mesh.shape["row"]),
        mesh=mesh,
        in_specs=(
            P(None, ("rhs", "row"), None),
            P(),
            P(),
            P(None, "row", None),
            P(None, "row", None),
            P(),
            P(),
        ),
        out_specs=P(None, "rhs", "row"),
        check_vma=False,
    )
```

```python
import functools

import jax
import jax.numpy as jnp
from jax import lax
from jax.experimental import pallas as pl
from jax.experimental.pallas import tpu as pltpu
from jax.sharding import PartitionSpec as P

LANES = 128
SHIFT = 8
WIDTH = 1 << SHIFT
MESH = pl.DeviceIdType.MESH


def split_matrix(matrix, high, low):
    depth = matrix.shape[2]
    for part in range(2):
        columns = slice(part * depth, (part + 1) * depth)
        values = matrix[part]
        rounded = values.astype(jnp.bfloat16)
        high[:, columns] = rounded
        low[:, columns] = (values - rounded.astype(jnp.float32)).astype(jnp.bfloat16)


def complex_product(operand, high, low):
    groups, size, depth = operand.shape
    half = size // 2
    swapped = pltpu.roll(operand, half, axis=1)
    is_real = lax.broadcasted_iota(jnp.int32, operand.shape, 1) < half
    swapped = jnp.where(is_real, -swapped, swapped)
    rows = groups * size
    wide = jnp.concatenate(
        [operand.reshape(rows, depth), swapped.reshape(rows, depth)], axis=1
    )
    top = wide.astype(jnp.bfloat16).astype(jnp.float32)
    both = jnp.concatenate([top, wide - top], axis=0).astype(jnp.bfloat16)
    contract = (((1,), (1,)), ((), ()))
    main = lax.dot_general(both, high[...], contract, preferred_element_type=jnp.float32)
    first = both[:rows] if rows % 16 == 0 else both
    rest = lax.dot_general(first, low[...], contract, preferred_element_type=jnp.float32)
    return (main[:rows] + main[rows:] + rest[:rows]).reshape(groups, size, depth)


def kernel(
    axis,
    count,
    owners_in,
    pivots_in,
    rhs_in,
    panel_first,
    panel_second,
    inverse_first,
    inverse_second,
    out,
    owners,
    pivots,
    raw,
    values,
    table,
    permuted,
    current,
    updated,
    product,
    block_one,
    merged,
    from_sibling,
    returned,
    solution_zero,
    solution_one,
    factors,
    high,
    low,
    load_sem,
    send_sem,
    receive_sem,
):
    me = lax.axis_index(axis)
    half = raw.shape[1]
    length = raw.shape[2]
    block_size = permuted.shape[2]
    tiles = block_size // LANES
    pairs = count // 2
    chip = lax.div(me, 2)
    core = lax.rem(me, 2)
    sibling = me + 1 - 2 * core
    middle = pairs // 2
    side = lax.div(chip, middle)
    own_slot = core * pairs + chip

    loads = [pltpu.make_async_copy(rhs_in, raw, load_sem.at[4])]
    for place, source in enumerate((inverse_first, panel_first, inverse_second, panel_second)):
        loads.append(pltpu.make_async_copy(source, factors.at[place], load_sem.at[place]))
    small = [
        pltpu.make_async_copy(owners_in, owners, load_sem.at[5]),
        pltpu.make_async_copy(pivots_in, pivots, load_sem.at[6]),
    ]
    for load in small + loads[:2]:
        load.start()

    def each_chip(body):
        @pl.loop(0, middle)
        def _(step):
            body((1 - side) * middle + lax.rem(chip + step, middle))

        @pl.loop(1, middle)
        def _(step):
            body(side * middle + lax.rem(chip + step, middle))

    def each_chip_near_first(body):
        @pl.loop(1, middle)
        def _(step):
            body(side * middle + lax.rem(chip + step, middle))

        @pl.loop(0, middle)
        def _(step):
            body((1 - side) * middle + lax.rem(chip + step, middle))

    barrier = pltpu.get_barrier_semaphore()

    @pl.loop(1, count)
    def _(step):
        pl.semaphore_signal(
            barrier,
            inc=1,
            device_id={axis: lax.rem(me + step, count)},
            device_id_type=MESH,
        )

    def remote(phase, source, target, peer, send_slot, receive_slot):
        return pltpu.make_async_remote_copy(
            src_ref=source,
            dst_ref=target,
            send_sem=send_sem.at[phase, send_slot],
            recv_sem=receive_sem.at[phase, receive_slot],
            device_id={axis: peer},
            device_id_type=MESH,
        )

    def spread(phase, chunks):
        def direct(other):
            return remote(
                phase, chunks.at[own_slot], chunks.at[own_slot], 2 * other + core, other, own_slot
            )

        def relay(other):
            slot = core * pairs + other
            return remote(phase, chunks.at[slot], chunks.at[slot], sibling, pairs + other, slot)

        def begin():
            each_chip(lambda other: direct(other).start())
            relay(chip).start()

        def forward():
            def one(other):
                slot = core * pairs + other
                remote(
                    phase, chunks.at[slot], chunks.at[slot], 2 * other + core, other, slot
                ).wait_recv()
                relay(other).start()

            each_chip_near_first(one)

        def complete():
            @pl.loop(0, pairs)
            def _(other):
                slot = (1 - core) * pairs + other
                remote(
                    phase, chunks.at[slot], chunks.at[slot], sibling, pairs + other, slot
                ).wait_recv()

        def drain():
            each_chip(lambda other: direct(other).wait_send())

            @pl.loop(0, pairs)
            def _(other):
                relay(other).wait_send()

        return begin, forward, complete, drain

    def deal(target_chip, target_core):
        slot = target_core * pairs + target_chip
        return remote(
            2,
            permuted.at[slot],
            current.at[own_slot],
            2 * target_chip + target_core,
            slot,
            own_slot,
        )

    def hand_back(other):
        return remote(
            3, merged.at[other], returned.at[chip], 2 * other + core, other, chip
        )

    def pair_copy():
        return remote(
            3,
            product.at[pl.ds((1 - core) * pairs, pairs)],
            from_sibling,
            sibling,
            pairs,
            pairs,
        )

    def block_at(slot):
        block = jnp.int32(0)
        for j in range(count):
            block = jnp.where(owners[j] == slot, j, block)
        return block

    def gather(block):
        groups = length // WIDTH
        index = [pivots[pl.ds(block * tiles + t, 1), :] for t in range(tiles)]
        index = jnp.concatenate(index, axis=1)
        column = jnp.broadcast_to(index & (WIDTH - 1), (WIDTH, block_size))
        place = lax.broadcasted_iota(jnp.int32, (WIDTH, block_size), 0)
        chosen = jnp.where(column == place, 1.0, 0.0).astype(jnp.bfloat16)
        found = jnp.dot(table[...], chosen, preferred_element_type=jnp.float32)
        group = jnp.broadcast_to(lax.shift_right_logical(index, SHIFT), (2 * half, block_size))
        taken = jnp.zeros((2 * half, block_size), jnp.float32)
        for g in range(groups):
            top = found[g * 2 * half : (g + 1) * 2 * half]
            rest = found[(groups + g) * 2 * half : (groups + g + 1) * 2 * half]
            taken = jnp.where(group == g, top + rest, taken)
        return taken

    def prepare(place):
        loads[place + 1].wait()
        split_matrix(factors.at[place], high.at[place], low.at[place])

    def gather_pair(target_chip):
        for target_core in range(2):
            chunk = gather(block_at(2 * target_chip + target_core))
            permuted[target_core * pairs + target_chip] = chunk

    def deal_chip(step):
        near = lax.div(step, middle)
        target_side = (1 - side) * (1 - near) + side * near
        target_chip = target_side * middle + lax.rem(chip + 1 + step, middle)
        gather_pair(target_chip)
        for target_core in range(2):
            deal(target_chip, target_core).start()

    begin_zero, forward_zero, complete_zero, drain_zero = spread(0, solution_zero)
    begin_one, forward_one, complete_one, drain_one = spread(1, solution_one)

    for load in small:
        load.wait()
    loads[0].wait()
    groups = length // WIDTH
    for g in range(groups):
        columns = slice(g * WIDTH, (g + 1) * WIDTH)
        wide = jnp.concatenate([raw[0, :, columns], raw[1, :, columns]], axis=0)
        values[g * 2 * half : (g + 1) * 2 * half, :] = wide
    rounded = values[...].astype(jnp.bfloat16)
    rows = groups * 2 * half
    table[:rows] = rounded
    table[rows:] = (values[...] - rounded.astype(jnp.float32)).astype(jnp.bfloat16)
    prepare(0)
    for load in loads[2:]:
        load.start()
    solution_zero[own_slot] = complex_product(gather(0)[None], high.at[0], low.at[0])[0]
    pl.semaphore_wait(barrier, count - 1)
    begin_zero()

    @pl.loop(0, middle)
    def _(step):
        deal_chip(step)

    prepare(1)
    forward_zero()
    block_one[...] = gather(1)

    @pl.loop(middle, pairs - 2)
    def _(step):
        deal_chip(step)

    complete_zero()
    product[...] = complex_product(solution_zero[...], high.at[1], low.at[1])
    pair_copy().start()
    deal_chip(pairs - 2)
    pair_copy().wait_recv()
    mine = product[pl.ds(core * pairs, pairs)]
    theirs = jnp.full(mine.shape, block_at(sibling), jnp.int32) == 1
    merged[...] = jnp.where(theirs, from_sibling[...], mine)
    each_chip(lambda other: hand_back(other).start())
    returned[chip] = merged[chip]

    gather_pair(chip)
    deal(chip, 1 - core).start()
    current[own_slot] = permuted[own_slot]
    my_block = block_at(me)
    prepare(2)
    prepare(3)

    @pl.loop(1, pairs)
    def _(step):
        other = lax.rem(chip + step, pairs)
        remote(3, returned.at[other], returned.at[other], sibling, other, other).wait_recv()

    second = block_one[...] - returned[lax.div(owners[1], 2)]
    solution_one[own_slot] = complex_product(second[None], high.at[2], low.at[2])[0]
    begin_one()

    @pl.loop(1, count)
    def _(step):
        slot = lax.rem(own_slot + step, count)
        remote(2, current.at[slot], current.at[slot], sibling, slot, slot).wait_recv()

    before = current[...]
    block = jnp.full(before.shape, my_block, jnp.int32)
    updated[...] = jnp.where(block > 0, before - product[...], solution_zero[...])
    forward_one()

    def last_half(first):
        rows = pl.ds(first, pairs)
        one = solution_one[rows]
        before = updated[rows]
        block = jnp.full(before.shape, my_block, jnp.int32)
        after = before - complex_product(one, high.at[3], low.at[3])
        current[rows] = jnp.where(block > 1, after, jnp.where(block == 1, one, before))

    last_half(core * pairs)
    complete_one()
    last_half((1 - core) * pairs)
    for part in range(2):
        rows = slice(part * half, (part + 1) * half)
        both = [current[c * pairs : (c + 1) * pairs, rows, :] for c in range(2)]
        out[part] = jnp.concatenate(both, axis=1).reshape(count * half, block_size)

    drain_zero()
    drain_one()
    pair_copy().wait_send()
    each_chip(lambda other: hand_back(other).wait_send())

    @pl.loop(1, count)
    def _(step):
        slot = lax.rem(own_slot + step, count)
        deal(lax.rem(slot, pairs), lax.div(slot, pairs)).wait_send()


def shards(rhs_in, pivots, owners, panel_first, panel_second, inverse_first, inverse_second, *, count):
    parts, half, length = rhs_in.shape
    block_size = panel_first.shape[2]
    chunks = (count, parts * half, block_size)
    part_chunks = (count // 2, parts * half, block_size)
    return pl.pallas_call(
        functools.partial(kernel, "row", count),
        out_shape=jax.ShapeDtypeStruct((parts, count * half, block_size), jnp.float32),
        in_specs=[pl.BlockSpec(memory_space=pltpu.HBM)] * 7,
        out_specs=pl.BlockSpec(memory_space=pltpu.VMEM),
        scratch_shapes=[
            pltpu.SMEM((count,), jnp.int32),
            pltpu.VMEM((length // LANES, LANES), jnp.int32),
            pltpu.VMEM((parts, half, length), jnp.float32),
            pltpu.VMEM((parts * half * length // WIDTH, WIDTH), jnp.float32),
            pltpu.VMEM((2 * parts * half * length // WIDTH, WIDTH), jnp.bfloat16),
            pltpu.VMEM(chunks, jnp.float32),
            pltpu.VMEM(chunks, jnp.float32),
            pltpu.VMEM(chunks, jnp.float32),
            pltpu.VMEM(chunks, jnp.float32),
            pltpu.VMEM(chunks[1:], jnp.float32),
            pltpu.VMEM(part_chunks, jnp.float32),
            pltpu.VMEM(part_chunks, jnp.float32),
            pltpu.VMEM(part_chunks, jnp.float32),
            pltpu.VMEM(chunks, jnp.float32),
            pltpu.VMEM(chunks, jnp.float32),
            pltpu.VMEM((4, parts, block_size, block_size), jnp.float32),
            pltpu.VMEM((4, block_size, parts * block_size), jnp.bfloat16),
            pltpu.VMEM((4, block_size, parts * block_size), jnp.bfloat16),
            pltpu.SemaphoreType.DMA((7,)),
            pltpu.SemaphoreType.DMA((4, count)),
            pltpu.SemaphoreType.DMA((4, count)),
        ],
        compiler_params=pltpu.CompilerParams(
            collective_id=0, has_side_effects=True, vmem_limit_bytes=57 * 1024 * 1024
        ),
        cost_estimate=pl.CostEstimate(flops=4 * 10**9, bytes_accessed=9 * 10**6, transcendentals=0),
    )(
        owners,
        pivots.reshape(length // LANES, LANES),
        rhs_in,
        panel_first,
        panel_second,
        inverse_first,
        inverse_second,
    )


def solution(mesh):
    return jax.shard_map(
        functools.partial(shards, count=mesh.shape["row"]),
        mesh=mesh,
        in_specs=(
            P(None, ("rhs", "row"), None),
            P(),
            P(),
            P(None, "row", None),
            P(None, "row", None),
            P(),
            P(),
        ),
        out_specs=P(None, "rhs", "row"),
        check_vma=False,
    )
```

```python
import functools

import jax
import jax.numpy as jnp
from jax import lax
from jax.experimental import pallas as pl
from jax.experimental.pallas import tpu as pltpu
from jax.sharding import PartitionSpec as P

LANES = 128
SHIFT = 8
WIDTH = 1 << SHIFT
MESH = pl.DeviceIdType.MESH


def split_matrix(matrix, high, low):
    depth = matrix.shape[2]
    for part in range(2):
        columns = slice(part * depth, (part + 1) * depth)
        values = matrix[part]
        rounded = values.astype(jnp.bfloat16)
        high[:, columns] = rounded
        low[:, columns] = (values - rounded.astype(jnp.float32)).astype(jnp.bfloat16)


def complex_product(operand, high, low):
    groups, size, depth = operand.shape
    half = size // 2
    swapped = pltpu.roll(operand, half, axis=1)
    is_real = lax.broadcasted_iota(jnp.int32, operand.shape, 1) < half
    swapped = jnp.where(is_real, -swapped, swapped)
    rows = groups * size
    wide = jnp.concatenate(
        [operand.reshape(rows, depth), swapped.reshape(rows, depth)], axis=1
    )
    top = wide.astype(jnp.bfloat16).astype(jnp.float32)
    both = jnp.concatenate([top, wide - top], axis=0).astype(jnp.bfloat16)
    contract = (((1,), (1,)), ((), ()))
    main = lax.dot_general(both, high[...], contract, preferred_element_type=jnp.float32)
    first = both[:rows] if rows % 16 == 0 else both
    rest = lax.dot_general(first, low[...], contract, preferred_element_type=jnp.float32)
    return (main[:rows] + main[rows:] + rest[:rows]).reshape(groups, size, depth)


def kernel(
    axis,
    count,
    owners_in,
    pivots_in,
    rhs_in,
    panel_first,
    panel_second,
    inverse_first,
    inverse_second,
    out,
    owners,
    pivots,
    raw,
    values,
    table,
    permuted,
    current,
    updated,
    product,
    block_one,
    merged,
    from_sibling,
    returned,
    solution_zero,
    solution_one,
    factors,
    high,
    low,
    load_sem,
    send_sem,
    receive_sem,
):
    me = lax.axis_index(axis)
    half = raw.shape[1]
    length = raw.shape[2]
    block_size = permuted.shape[2]
    tiles = block_size // LANES
    pairs = count // 2
    chip = lax.div(me, 2)
    core = lax.rem(me, 2)
    sibling = me + 1 - 2 * core
    middle = pairs // 2
    side = lax.div(chip, middle)
    own_slot = core * pairs + chip

    loads = [pltpu.make_async_copy(rhs_in, raw, load_sem.at[4])]
    for place, source in enumerate((inverse_first, panel_first, inverse_second, panel_second)):
        loads.append(pltpu.make_async_copy(source, factors.at[place], load_sem.at[place]))
    small = [
        pltpu.make_async_copy(owners_in, owners, load_sem.at[5]),
        pltpu.make_async_copy(pivots_in, pivots, load_sem.at[6]),
    ]
    for load in small + loads[:2]:
        load.start()

    def each_chip(body):
        @pl.loop(0, middle)
        def _(step):
            body((1 - side) * middle + lax.rem(chip + step, middle))

        @pl.loop(1, middle)
        def _(step):
            body(side * middle + lax.rem(chip + step, middle))

    def each_chip_near_first(body):
        @pl.loop(1, middle)
        def _(step):
            body(side * middle + lax.rem(chip + step, middle))

        @pl.loop(0, middle)
        def _(step):
            body((1 - side) * middle + lax.rem(chip + step, middle))

    barrier = pltpu.get_barrier_semaphore()

    @pl.loop(1, count)
    def _(step):
        pl.semaphore_signal(
            barrier,
            inc=1,
            device_id={axis: lax.rem(me + step, count)},
            device_id_type=MESH,
        )

    def remote(phase, source, target, peer, send_slot, receive_slot):
        return pltpu.make_async_remote_copy(
            src_ref=source,
            dst_ref=target,
            send_sem=send_sem.at[phase, send_slot],
            recv_sem=receive_sem.at[phase, receive_slot],
            device_id={axis: peer},
            device_id_type=MESH,
        )

    def spread(phase, chunks):
        def direct(other):
            return remote(
                phase, chunks.at[own_slot], chunks.at[own_slot], 2 * other + core, other, own_slot
            )

        def relay(other):
            slot = core * pairs + other
            return remote(phase, chunks.at[slot], chunks.at[slot], sibling, pairs + other, slot)

        def begin():
            each_chip(lambda other: direct(other).start())
            relay(chip).start()

        def forward():
            def one(other):
                slot = core * pairs + other
                remote(
                    phase, chunks.at[slot], chunks.at[slot], 2 * other + core, other, slot
                ).wait_recv()
                relay(other).start()

            each_chip_near_first(one)

        def complete():
            @pl.loop(0, pairs)
            def _(other):
                slot = (1 - core) * pairs + other
                remote(
                    phase, chunks.at[slot], chunks.at[slot], sibling, pairs + other, slot
                ).wait_recv()

        def drain():
            each_chip(lambda other: direct(other).wait_send())

            @pl.loop(0, pairs)
            def _(other):
                relay(other).wait_send()

        return begin, forward, complete, drain

    def deal(target_chip, target_core):
        slot = target_core * pairs + target_chip
        return remote(
            2,
            permuted.at[slot],
            current.at[own_slot],
            2 * target_chip + target_core,
            slot,
            own_slot,
        )

    def hand_back(other):
        return remote(
            3, merged.at[other], returned.at[chip], 2 * other + core, other, chip
        )

    def pair_copy():
        return remote(
            3,
            product.at[pl.ds((1 - core) * pairs, pairs)],
            from_sibling,
            sibling,
            pairs,
            pairs,
        )

    def block_at(slot):
        block = jnp.int32(0)
        for j in range(count):
            block = jnp.where(owners[j] == slot, j, block)
        return block

    def gather(block):
        groups = length // WIDTH
        index = [pivots[pl.ds(block * tiles + t, 1), :] for t in range(tiles)]
        index = jnp.concatenate(index, axis=1)
        column = jnp.broadcast_to(index & (WIDTH - 1), (WIDTH, block_size))
        place = lax.broadcasted_iota(jnp.int32, (WIDTH, block_size), 0)
        chosen = jnp.where(column == place, 1.0, 0.0).astype(jnp.bfloat16)
        found = jnp.dot(table[...], chosen, preferred_element_type=jnp.float32)
        group = jnp.broadcast_to(lax.shift_right_logical(index, SHIFT), (2 * half, block_size))
        taken = jnp.zeros((2 * half, block_size), jnp.float32)
        for g in range(groups):
            top = found[g * 2 * half : (g + 1) * 2 * half]
            rest = found[(groups + g) * 2 * half : (groups + g + 1) * 2 * half]
            taken = jnp.where(group == g, top + rest, taken)
        return taken

    def prepare(place):
        loads[place + 1].wait()
        split_matrix(factors.at[place], high.at[place], low.at[place])

    def gather_pair(target_chip):
        for target_core in range(2):
            chunk = gather(block_at(2 * target_chip + target_core))
            permuted[target_core * pairs + target_chip] = chunk

    def deal_chip(step):
        near = lax.div(step, middle)
        target_side = (1 - side) * (1 - near) + side * near
        target_chip = target_side * middle + lax.rem(chip + 1 + step, middle)
        gather_pair(target_chip)
        for target_core in range(2):
            deal(target_chip, target_core).start()

    begin_zero, forward_zero, complete_zero, drain_zero = spread(0, solution_zero)
    begin_one, forward_one, complete_one, drain_one = spread(1, solution_one)

    for load in small:
        load.wait()
    loads[0].wait()
    groups = length // WIDTH
    for g in range(groups):
        columns = slice(g * WIDTH, (g + 1) * WIDTH)
        wide = jnp.concatenate([raw[0, :, columns], raw[1, :, columns]], axis=0)
        values[g * 2 * half : (g + 1) * 2 * half, :] = wide
    rounded = values[...].astype(jnp.bfloat16)
    rows = groups * 2 * half
    table[:rows] = rounded
    table[rows:] = (values[...] - rounded.astype(jnp.float32)).astype(jnp.bfloat16)
    prepare(0)
    for load in loads[2:]:
        load.start()
    solution_zero[own_slot] = complex_product(gather(0)[None], high.at[0], low.at[0])[0]
    pl.semaphore_wait(barrier, count - 1)
    begin_zero()

    @pl.loop(0, middle)
    def _(step):
        deal_chip(step)

    prepare(1)
    forward_zero()
    block_one[...] = gather(1)

    complete_zero()
    product[...] = complex_product(solution_zero[...], high.at[1], low.at[1])
    pair_copy().start()
    deal_chip(middle)
    pair_copy().wait_recv()
    mine = product[pl.ds(core * pairs, pairs)]
    theirs = jnp.full(mine.shape, block_at(sibling), jnp.int32) == 1
    merged[...] = jnp.where(theirs, from_sibling[...], mine)
    each_chip(lambda other: hand_back(other).start())
    returned[chip] = merged[chip]

    @pl.loop(middle + 1, pairs - 1)
    def _(step):
        deal_chip(step)

    prepare(2)
    gather_pair(chip)
    deal(chip, 1 - core).start()
    current[own_slot] = permuted[own_slot]
    my_block = block_at(me)

    @pl.loop(1, pairs)
    def _(step):
        other = lax.rem(chip + step, pairs)
        remote(3, returned.at[other], returned.at[other], sibling, other, other).wait_recv()

    second = block_one[...] - returned[lax.div(owners[1], 2)]
    solution_one[own_slot] = complex_product(second[None], high.at[2], low.at[2])[0]
    begin_one()

    @pl.loop(1, count)
    def _(step):
        slot = lax.rem(own_slot + step, count)
        remote(2, current.at[slot], current.at[slot], sibling, slot, slot).wait_recv()

    before = current[...]
    block = jnp.full(before.shape, my_block, jnp.int32)
    updated[...] = jnp.where(block > 0, before - product[...], solution_zero[...])
    prepare(3)
    forward_one()
    drain_zero()
    pair_copy().wait_send()
    each_chip(lambda other: hand_back(other).wait_send())

    @pl.loop(1, count)
    def _(step):
        slot = lax.rem(own_slot + step, count)
        deal(lax.rem(slot, pairs), lax.div(slot, pairs)).wait_send()

    def last_half(first):
        rows = pl.ds(first, pairs)
        one = solution_one[rows]
        before = updated[rows]
        block = jnp.full(before.shape, my_block, jnp.int32)
        after = before - complex_product(one, high.at[3], low.at[3])
        current[rows] = jnp.where(block > 1, after, jnp.where(block == 1, one, before))

    last_half(core * pairs)
    complete_one()
    last_half((1 - core) * pairs)
    for part in range(2):
        rows = slice(part * half, (part + 1) * half)
        both = [current[c * pairs : (c + 1) * pairs, rows, :] for c in range(2)]
        out[part] = jnp.concatenate(both, axis=1).reshape(count * half, block_size)

    drain_one()


def shards(rhs_in, pivots, owners, panel_first, panel_second, inverse_first, inverse_second, *, count):
    parts, half, length = rhs_in.shape
    block_size = panel_first.shape[2]
    chunks = (count, parts * half, block_size)
    part_chunks = (count // 2, parts * half, block_size)
    return pl.pallas_call(
        functools.partial(kernel, "row", count),
        out_shape=jax.ShapeDtypeStruct((parts, count * half, block_size), jnp.float32),
        in_specs=[pl.BlockSpec(memory_space=pltpu.HBM)] * 7,
        out_specs=pl.BlockSpec(memory_space=pltpu.VMEM),
        scratch_shapes=[
            pltpu.SMEM((count,), jnp.int32),
            pltpu.VMEM((length // LANES, LANES), jnp.int32),
            pltpu.VMEM((parts, half, length), jnp.float32),
            pltpu.VMEM((parts * half * length // WIDTH, WIDTH), jnp.float32),
            pltpu.VMEM((2 * parts * half * length // WIDTH, WIDTH), jnp.bfloat16),
            pltpu.VMEM(chunks, jnp.float32),
            pltpu.VMEM(chunks, jnp.float32),
            pltpu.VMEM(chunks, jnp.float32),
            pltpu.VMEM(chunks, jnp.float32),
            pltpu.VMEM(chunks[1:], jnp.float32),
            pltpu.VMEM(part_chunks, jnp.float32),
            pltpu.VMEM(part_chunks, jnp.float32),
            pltpu.VMEM(part_chunks, jnp.float32),
            pltpu.VMEM(chunks, jnp.float32),
            pltpu.VMEM(chunks, jnp.float32),
            pltpu.VMEM((4, parts, block_size, block_size), jnp.float32),
            pltpu.VMEM((4, block_size, parts * block_size), jnp.bfloat16),
            pltpu.VMEM((4, block_size, parts * block_size), jnp.bfloat16),
            pltpu.SemaphoreType.DMA((7,)),
            pltpu.SemaphoreType.DMA((4, count)),
            pltpu.SemaphoreType.DMA((4, count)),
        ],
        compiler_params=pltpu.CompilerParams(
            collective_id=0, has_side_effects=True, vmem_limit_bytes=57 * 1024 * 1024
        ),
        cost_estimate=pl.CostEstimate(flops=4 * 10**9, bytes_accessed=9 * 10**6, transcendentals=0),
    )(
        owners,
        pivots.reshape(length // LANES, LANES),
        rhs_in,
        panel_first,
        panel_second,
        inverse_first,
        inverse_second,
    )


def solution(mesh):
    return jax.shard_map(
        functools.partial(shards, count=mesh.shape["row"]),
        mesh=mesh,
        in_specs=(
            P(None, ("rhs", "row"), None),
            P(),
            P(),
            P(None, "row", None),
            P(None, "row", None),
            P(),
            P(),
        ),
        out_specs=P(None, "rhs", "row"),
        check_vma=False,
    )
```

```python
import functools

import jax
import jax.numpy as jnp
from jax import lax
from jax.experimental import pallas as pl
from jax.experimental.pallas import tpu as pltpu
from jax.sharding import PartitionSpec as P

LANES = 128
SHIFT = 8
WIDTH = 1 << SHIFT
MESH = pl.DeviceIdType.MESH


def split_matrix(matrix, high, low):
    depth = matrix.shape[2]
    for part in range(2):
        columns = slice(part * depth, (part + 1) * depth)
        values = matrix[part]
        rounded = values.astype(jnp.bfloat16)
        high[:, columns] = rounded
        low[:, columns] = (values - rounded.astype(jnp.float32)).astype(jnp.bfloat16)


def complex_product(operand, high, low):
    groups, size, depth = operand.shape
    half = size // 2
    swapped = pltpu.roll(operand, half, axis=1)
    is_real = lax.broadcasted_iota(jnp.int32, operand.shape, 1) < half
    swapped = jnp.where(is_real, -swapped, swapped)
    rows = groups * size
    wide = jnp.concatenate(
        [operand.reshape(rows, depth), swapped.reshape(rows, depth)], axis=1
    )
    top = wide.astype(jnp.bfloat16).astype(jnp.float32)
    both = jnp.concatenate([top, wide - top], axis=0).astype(jnp.bfloat16)
    contract = (((1,), (1,)), ((), ()))
    main = lax.dot_general(both, high[...], contract, preferred_element_type=jnp.float32)
    first = both[:rows] if rows % 16 == 0 else both
    rest = lax.dot_general(first, low[...], contract, preferred_element_type=jnp.float32)
    return (main[:rows] + main[rows:] + rest[:rows]).reshape(groups, size, depth)


def kernel(
    axis,
    count,
    owners_in,
    pivots_in,
    rhs_in,
    panel_first,
    panel_second,
    inverse_first,
    inverse_second,
    out,
    owners,
    pivots,
    raw,
    values,
    table,
    permuted,
    current,
    updated,
    product,
    block_one,
    merged,
    from_sibling,
    returned,
    solution_zero,
    solution_one,
    factors,
    high,
    low,
    load_sem,
    send_sem,
    receive_sem,
):
    me = lax.axis_index(axis)
    half = raw.shape[1]
    length = raw.shape[2]
    block_size = permuted.shape[2]
    tiles = block_size // LANES
    pairs = count // 2
    chip = lax.div(me, 2)
    core = lax.rem(me, 2)
    sibling = me + 1 - 2 * core
    middle = pairs // 2
    side = lax.div(chip, middle)
    own_slot = core * pairs + chip

    loads = [pltpu.make_async_copy(rhs_in, raw, load_sem.at[4])]
    for place, source in enumerate((inverse_first, panel_first, inverse_second, panel_second)):
        loads.append(pltpu.make_async_copy(source, factors.at[place], load_sem.at[place]))
    small = [
        pltpu.make_async_copy(owners_in, owners, load_sem.at[5]),
        pltpu.make_async_copy(pivots_in, pivots, load_sem.at[6]),
    ]
    for load in small + loads[:2]:
        load.start()

    def each_chip(body):
        @pl.loop(0, middle)
        def _(step):
            body((1 - side) * middle + lax.rem(chip + step, middle))

        @pl.loop(1, middle)
        def _(step):
            body(side * middle + lax.rem(chip + step, middle))

    def each_chip_near_first(body):
        @pl.loop(1, middle)
        def _(step):
            body(side * middle + lax.rem(chip + step, middle))

        @pl.loop(0, middle)
        def _(step):
            body((1 - side) * middle + lax.rem(chip + step, middle))

    barrier = pltpu.get_barrier_semaphore()

    @pl.loop(1, count)
    def _(step):
        pl.semaphore_signal(
            barrier,
            inc=1,
            device_id={axis: lax.rem(me + step, count)},
            device_id_type=MESH,
        )

    def remote(phase, source, target, peer, send_slot, receive_slot):
        return pltpu.make_async_remote_copy(
            src_ref=source,
            dst_ref=target,
            send_sem=send_sem.at[phase, send_slot],
            recv_sem=receive_sem.at[phase, receive_slot],
            device_id={axis: peer},
            device_id_type=MESH,
        )

    def spread(phase, chunks):
        def direct(other):
            return remote(
                phase, chunks.at[own_slot], chunks.at[own_slot], 2 * other + core, other, own_slot
            )

        def relay(other):
            slot = core * pairs + other
            return remote(phase, chunks.at[slot], chunks.at[slot], sibling, pairs + other, slot)

        def begin():
            each_chip(lambda other: direct(other).start())
            relay(chip).start()

        def forward():
            def one(other):
                slot = core * pairs + other
                remote(
                    phase, chunks.at[slot], chunks.at[slot], 2 * other + core, other, slot
                ).wait_recv()
                relay(other).start()

            each_chip_near_first(one)

        def complete():
            @pl.loop(0, pairs)
            def _(other):
                slot = (1 - core) * pairs + other
                remote(
                    phase, chunks.at[slot], chunks.at[slot], sibling, pairs + other, slot
                ).wait_recv()

        def drain():
            each_chip(lambda other: direct(other).wait_send())

            @pl.loop(0, pairs)
            def _(other):
                relay(other).wait_send()

        return begin, forward, complete, drain

    def deal(target_chip, target_core):
        slot = target_core * pairs + target_chip
        return remote(
            2,
            permuted.at[slot],
            current.at[own_slot],
            2 * target_chip + target_core,
            slot,
            own_slot,
        )

    def hand_back(other):
        return remote(
            3, merged.at[other], returned.at[chip], 2 * other + core, other, chip
        )

    def pair_copy():
        return remote(
            3,
            product.at[pl.ds((1 - core) * pairs, pairs)],
            from_sibling,
            sibling,
            pairs,
            pairs,
        )

    def block_at(slot):
        block = jnp.int32(0)
        for j in range(count):
            block = jnp.where(owners[j] == slot, j, block)
        return block

    def gather(block):
        groups = length // WIDTH
        index = [pivots[pl.ds(block * tiles + t, 1), :] for t in range(tiles)]
        index = jnp.concatenate(index, axis=1)
        column = jnp.broadcast_to(index & (WIDTH - 1), (WIDTH, block_size))
        place = lax.broadcasted_iota(jnp.int32, (WIDTH, block_size), 0)
        chosen = jnp.where(column == place, 1.0, 0.0).astype(jnp.bfloat16)
        found = jnp.dot(table[...], chosen, preferred_element_type=jnp.float32)
        group = jnp.broadcast_to(lax.shift_right_logical(index, SHIFT), (2 * half, block_size))
        taken = jnp.zeros((2 * half, block_size), jnp.float32)
        for g in range(groups):
            top = found[g * 2 * half : (g + 1) * 2 * half]
            rest = found[(groups + g) * 2 * half : (groups + g + 1) * 2 * half]
            taken = jnp.where(group == g, top + rest, taken)
        return taken

    def prepare(place):
        loads[place + 1].wait()
        split_matrix(factors.at[place], high.at[place], low.at[place])

    def gather_pair(target_chip):
        for target_core in range(2):
            chunk = gather(block_at(2 * target_chip + target_core))
            permuted[target_core * pairs + target_chip] = chunk

    def deal_chip(step):
        near = lax.div(step, middle)
        target_side = (1 - side) * (1 - near) + side * near
        target_chip = target_side * middle + lax.rem(chip + 1 + step, middle)
        gather_pair(target_chip)
        for target_core in range(2):
            deal(target_chip, target_core).start()

    begin_zero, forward_zero, complete_zero, drain_zero = spread(0, solution_zero)
    begin_one, forward_one, complete_one, drain_one = spread(1, solution_one)

    for load in small:
        load.wait()
    loads[0].wait()
    groups = length // WIDTH
    for g in range(groups):
        columns = slice(g * WIDTH, (g + 1) * WIDTH)
        wide = jnp.concatenate([raw[0, :, columns], raw[1, :, columns]], axis=0)
        values[g * 2 * half : (g + 1) * 2 * half, :] = wide
    rounded = values[...].astype(jnp.bfloat16)
    rows = groups * 2 * half
    table[:rows] = rounded
    table[rows:] = (values[...] - rounded.astype(jnp.float32)).astype(jnp.bfloat16)
    prepare(0)
    for load in loads[2:]:
        load.start()
    solution_zero[own_slot] = complex_product(gather(0)[None], high.at[0], low.at[0])[0]
    pl.semaphore_wait(barrier, count - 1)
    begin_zero()

    @pl.loop(0, middle)
    def _(step):
        deal_chip(step)

    prepare(1)
    forward_zero()
    block_one[...] = gather(1)

    complete_zero()

    def update_half(first):
        rows = pl.ds(first, pairs)
        product[rows] = complex_product(solution_zero[rows], high.at[1], low.at[1])

    update_half((1 - core) * pairs)
    pair_copy().start()
    update_half(core * pairs)
    pair_copy().wait_recv()
    mine = product[pl.ds(core * pairs, pairs)]
    theirs = jnp.full(mine.shape, block_at(sibling), jnp.int32) == 1
    merged[...] = jnp.where(theirs, from_sibling[...], mine)
    each_chip(lambda other: hand_back(other).start())
    returned[chip] = merged[chip]

    @pl.loop(middle, pairs - 1)
    def _(step):
        deal_chip(step)

    prepare(2)
    gather_pair(chip)
    deal(chip, 1 - core).start()
    current[own_slot] = permuted[own_slot]
    my_block = block_at(me)

    @pl.loop(1, pairs)
    def _(step):
        other = lax.rem(chip + step, pairs)
        remote(3, returned.at[other], returned.at[other], sibling, other, other).wait_recv()

    second = block_one[...] - returned[lax.div(owners[1], 2)]
    solution_one[own_slot] = complex_product(second[None], high.at[2], low.at[2])[0]
    begin_one()

    @pl.loop(1, count)
    def _(step):
        slot = lax.rem(own_slot + step, count)
        remote(2, current.at[slot], current.at[slot], sibling, slot, slot).wait_recv()

    before = current[...]
    block = jnp.full(before.shape, my_block, jnp.int32)
    updated[...] = jnp.where(block > 0, before - product[...], solution_zero[...])
    prepare(3)
    forward_one()
    drain_zero()
    pair_copy().wait_send()
    each_chip(lambda other: hand_back(other).wait_send())

    @pl.loop(1, count)
    def _(step):
        slot = lax.rem(own_slot + step, count)
        deal(lax.rem(slot, pairs), lax.div(slot, pairs)).wait_send()

    def last_half(first):
        rows = pl.ds(first, pairs)
        one = solution_one[rows]
        before = updated[rows]
        block = jnp.full(before.shape, my_block, jnp.int32)
        after = before - complex_product(one, high.at[3], low.at[3])
        current[rows] = jnp.where(block > 1, after, jnp.where(block == 1, one, before))

    last_half(core * pairs)
    complete_one()
    last_half((1 - core) * pairs)
    for part in range(2):
        rows = slice(part * half, (part + 1) * half)
        both = [current[c * pairs : (c + 1) * pairs, rows, :] for c in range(2)]
        out[part] = jnp.concatenate(both, axis=1).reshape(count * half, block_size)

    drain_one()


def shards(rhs_in, pivots, owners, panel_first, panel_second, inverse_first, inverse_second, *, count):
    parts, half, length = rhs_in.shape
    block_size = panel_first.shape[2]
    chunks = (count, parts * half, block_size)
    part_chunks = (count // 2, parts * half, block_size)
    return pl.pallas_call(
        functools.partial(kernel, "row", count),
        out_shape=jax.ShapeDtypeStruct((parts, count * half, block_size), jnp.float32),
        in_specs=[pl.BlockSpec(memory_space=pltpu.HBM)] * 7,
        out_specs=pl.BlockSpec(memory_space=pltpu.VMEM),
        scratch_shapes=[
            pltpu.SMEM((count,), jnp.int32),
            pltpu.VMEM((length // LANES, LANES), jnp.int32),
            pltpu.VMEM((parts, half, length), jnp.float32),
            pltpu.VMEM((parts * half * length // WIDTH, WIDTH), jnp.float32),
            pltpu.VMEM((2 * parts * half * length // WIDTH, WIDTH), jnp.bfloat16),
            pltpu.VMEM(chunks, jnp.float32),
            pltpu.VMEM(chunks, jnp.float32),
            pltpu.VMEM(chunks, jnp.float32),
            pltpu.VMEM(chunks, jnp.float32),
            pltpu.VMEM(chunks[1:], jnp.float32),
            pltpu.VMEM(part_chunks, jnp.float32),
            pltpu.VMEM(part_chunks, jnp.float32),
            pltpu.VMEM(part_chunks, jnp.float32),
            pltpu.VMEM(chunks, jnp.float32),
            pltpu.VMEM(chunks, jnp.float32),
            pltpu.VMEM((4, parts, block_size, block_size), jnp.float32),
            pltpu.VMEM((4, block_size, parts * block_size), jnp.bfloat16),
            pltpu.VMEM((4, block_size, parts * block_size), jnp.bfloat16),
            pltpu.SemaphoreType.DMA((7,)),
            pltpu.SemaphoreType.DMA((4, count)),
            pltpu.SemaphoreType.DMA((4, count)),
        ],
        compiler_params=pltpu.CompilerParams(
            collective_id=0, has_side_effects=True, vmem_limit_bytes=57 * 1024 * 1024
        ),
        cost_estimate=pl.CostEstimate(flops=4 * 10**9, bytes_accessed=9 * 10**6, transcendentals=0),
    )(
        owners,
        pivots.reshape(length // LANES, LANES),
        rhs_in,
        panel_first,
        panel_second,
        inverse_first,
        inverse_second,
    )


def solution(mesh):
    return jax.shard_map(
        functools.partial(shards, count=mesh.shape["row"]),
        mesh=mesh,
        in_specs=(
            P(None, ("rhs", "row"), None),
            P(),
            P(),
            P(None, "row", None),
            P(None, "row", None),
            P(),
            P(),
        ),
        out_specs=P(None, "rhs", "row"),
        check_vma=False,
    )
```
